512 devices in a mesh: expert: 16 (over y, core), replica: 32 (over x, z).
Axes of the slice: x: 4, y: 8, z: 8, core: 2. Of those that a mesh axis runs over, the one named last changes fastest.
Arguments:
- out_grad: bfloat16 [32, 4096, 4096], P('replica', 'expert'), may hold values from -0.25 to 0.25
- hidden: bfloat16 [32, 16, 128, 1536], P('replica', 'expert'), may hold values from -6 to 6
- token_index: int32 [32, 16, 128], P('replica', None, 'expert'), may hold values from 0 to 4095, as said below
- router_gate: float32 [32, 16, 128], P('replica', None, 'expert'), may hold values from 0.05 to 1
- valid_count: int32 [32, 16, 16], P('replica', None, 'expert'), may hold values from 4 to 8, as said below
- q_previous: float32 [16, 1536, 32], P('expert'), may hold values from -6 to 6
Outputs:
- p_factor: float32 [16, 4096, 32], P('expert')
- q_factor: float32 [16, 1536, 32], P('expert')
The draws below stay inside these ranges and needn't reach their ends.
Inputs may be any that keep to these rules, and one draw needn't show every extreme that they name: `token_index`: padded row k of an expert names a token of the block held by expert-axis index k div 8, that is one in [(k div 8) * 256, (k div 8 + 1) * 256); rows that live marks 0 may name any token of that block. `valid_count`: in each replica group some expert has 8 live rows from every device.
All inputs are finite; a program needn't handle non-finite values.
Results may differ from the reference program's by a relative error of at most 0.0029.
Values may be sent and summed in bfloat16 or wider, within the bound.
A program may use at most 128 MiB of HBM per device.

```python
import math
import jax
import jax.numpy as jnp
from jax import lax

D = 4096
F = 1536
RANK = 32
SLOT = 8
TOK_DEV = 256
EXPERTS = 16
CAP = 128
GROUP = 4096
REPLICAS = 32
N_EXPERT = 16


def draw_token_index(key, part):
    key = jax.random.fold_in(key, 11)
    base_key, step_key = jax.random.split(key)
    draw_shape = (REPLICAS, EXPERTS, N_EXPERT, 1)
    offset = jax.random.randint(base_key, draw_shape, 0, TOK_DEV)
    stride = 2 * jax.random.randint(step_key, draw_shape, 0, max(TOK_DEV // 2, 1)) + 1
    within = (offset + stride * jnp.arange(SLOT, dtype=jnp.int32)) % TOK_DEV
    block_start = (jnp.arange(N_EXPERT, dtype=jnp.int32) * TOK_DEV)[None, None, :, None]
    return (within + block_start).reshape(REPLICAS, EXPERTS, CAP).astype(jnp.int32)


def draw_valid_count(key, part):
    key = jax.random.fold_in(key, 12)
    first_key, second_key, full_key = jax.random.split(key, 3)
    draw_shape = (REPLICAS, EXPERTS, N_EXPERT)
    missing = jax.random.randint(first_key, draw_shape, 0, SLOT + 1) * jax.random.randint(second_key, draw_shape, 0, SLOT + 1) // (2 * SLOT)
    counts = SLOT - missing
    full_expert = jax.random.randint(full_key, (REPLICAS, 1, 1), 0, EXPERTS)
    experts_iota = jnp.arange(EXPERTS, dtype=jnp.int32)[None, :, None]
    return jnp.where(experts_iota == full_expert, SLOT, counts).astype(jnp.int32)


def levels(rng, dims, cuts, smallest, largest):
    factor_of, own = 1.0, jax.random.fold_in(rng, 6)
    for dim, shards_of in cuts:
        draws = jnp.exp(jax.random.uniform(jax.random.fold_in(own, dim), (shards_of,), jnp.float32, smallest / len(cuts), largest / len(cuts)))
        factor_of = factor_of * jnp.repeat(draws, dims[dim] // shards_of).reshape([-1 if axis == dim else 1 for axis in range(len(dims))])
    return factor_of


def centred(rng, dims, scale, limit, pieces=(), held_as=jnp.bfloat16):
    values = jax.random.normal(rng, dims, jnp.float32) * scale
    if len(pieces) > 0:
        values = levels(rng, dims, pieces, -0.22, 0.18) * values
    return jnp.clip(values, min=-limit, max=limit).astype(held_as)


def setup_inputs(seed: int = 0) -> dict:
    streams_of = jax.random.split(jax.random.key(seed), 7)
    out_grad = centred(streams_of[0], (REPLICAS, GROUP, D), 0.03125, 0.25, ((0, 32), (1, 16)))
    hidden = centred(streams_of[1], (REPLICAS, EXPERTS, CAP, F), 1.0, 6.0, ((0, 32), (1, 16)))
    token_index = draw_token_index(jax.random.fold_in(streams_of[6], 71), 0)
    router_gate = jnp.clip(0.05 + 0.95 * jax.random.uniform(streams_of[3], (REPLICAS, EXPERTS, CAP), jnp.float32) ** levels(streams_of[3], (REPLICAS, EXPERTS, CAP), ((0, 32), (2, 16)), -0.2, 0.2), 0.05, 1.0)
    valid_count = draw_valid_count(jax.random.fold_in(streams_of[6], 71), 0)
    q_previous = centred(streams_of[5], (EXPERTS, F, RANK), 1.0, 6.0, ((0, 16),), jnp.float32)
    return dict(out_grad=out_grad, hidden=hidden, token_index=token_index, router_gate=router_gate, valid_count=valid_count, q_previous=q_previous)


def contract_rows(left_mat, right_mat):
    return lax.dot_general(left_mat.astype(jnp.float32), right_mat.astype(jnp.float32), (((0,), (0,)), ((), ())), precision=lax.Precision.HIGHEST, preferred_element_type=jnp.float32)

def orthonormal(matrix):
    gram_matrix = contract_rows(matrix, matrix)
    lower_factor = jnp.linalg.cholesky(gram_matrix)
    return lax.linalg.triangular_solve(lower_factor, matrix, left_side=False, lower=True, transpose_a=True)

def reference(out_grad, hidden, token_index, router_gate, valid_count, q_previous):
    positions = jnp.arange(CAP, dtype=jnp.int32)
    sources = positions // SLOT
    live_slots = (positions % SLOT)[None, None, :] < valid_count[:, :, sources]
    weights = jnp.where(live_slots, router_gate, jnp.zeros_like(router_gate))

    def one_expert(expert):
        chosen = token_index[:, expert]
        picked = jax.vmap(lambda grads, picks: jnp.take(grads, picks, axis=0))(out_grad, chosen)
        routed = (picked.astype(jnp.float32) * weights[:, expert][:, :, None]).astype(jnp.bfloat16)
        routed_rows = routed.reshape(REPLICAS * CAP, D).astype(jnp.float32)
        activation = hidden[:, expert].reshape(REPLICAS * CAP, F).astype(jnp.float32)
        basis_prior = q_previous[expert]
        p_sum = contract_rows(routed_rows, jnp.dot(activation.astype(jnp.float32), basis_prior.astype(jnp.float32), precision=lax.Precision.HIGHEST, preferred_element_type=jnp.float32))
        ortho_basis = orthonormal(p_sum)
        q_new = contract_rows(activation, jnp.dot(routed_rows.astype(jnp.float32), ortho_basis.astype(jnp.float32), precision=lax.Precision.HIGHEST, preferred_element_type=jnp.float32))
        return (ortho_basis * math.sqrt(D), q_new)
    p_factor, q_factor = lax.map(one_expert, jnp.arange(EXPERTS, dtype=jnp.int32))
    return (p_factor, q_factor)
```

```python
import math

import jax
import jax.numpy as jnp
from jax import lax
from jax.experimental import pallas as pl
from jax.experimental.pallas import tpu as pltpu
from jax.sharding import PartitionSpec as P

MESH = pl.DeviceIdType.MESH
F32, BF16 = jnp.float32, jnp.bfloat16

D, F, RANK, SLOT, TOK = 4096, 1536, 32, 8, 256
NE, NR = 16, 32
NX, NZ, NY = 4, 8, 8
CH = 4
HALF = D // 2
W = HALF // CH
QOWN = 24


def split2(v):
    hi = v.astype(BF16)
    return hi, (v - hi.astype(F32)).astype(BF16)


def far_first(i, n):
    return lax.rem(n // 2 + (1 - 2 * lax.rem(i, 2)) * ((i + 1) // 2) + n, n)


def dot_nt(a, b):
    return lax.dot_general(a, b, (((1,), (1,)), ((), ())), preferred_element_type=F32)


def body(
    x_hbm, h_hbm, q_hbm, idx_ref, gate_ref, valid_ref,
    p_out, q_out,
    xv, hv, qv, sbuf, rbuf, psend, prs, pag, qsend, qrs, qag,
    load_sem, row_s, row_r, prs_s, prs_r, pag_s, pag_r, qrs_s, qrs_r, qag_s, qag_r,
):
    e = lax.axis_index("expert")
    r = lax.axis_index("replica")
    y, core = e // 2, lax.rem(e, 2)
    gx, gz = r // NZ, lax.rem(r, NZ)

    def expert_peer(i):
        to = lax.rem(y + far_first(i // 2, NY), NY)
        return to * 2 + lax.rem(core + 1 - lax.rem(i, 2), 2)

    def replica_peer(i):
        to_z = lax.rem(gz + far_first(i // NX, NZ), NZ)
        to_x = lax.rem(gx + far_first(lax.rem(i, NX), NX), NX)
        return to_x * NZ + to_z

    barrier = pltpu.get_barrier_semaphore()

    def greet_e(i, c):
        pl.semaphore_signal(barrier, inc=1, device_id=(expert_peer(i), r), device_id_type=MESH)
        return c

    def greet_r(i, c):
        pl.semaphore_signal(barrier, inc=1, device_id=(e, replica_peer(i)), device_id_type=MESH)
        return c

    lax.fori_loop(0, NE - 1, greet_e, 0)
    lax.fori_loop(0, NR - 1, greet_r, 0)

    loads = []
    for c in range(CH):
        for h in range(2):
            cp = pltpu.make_async_copy(
                x_hbm.at[:, pl.ds(h * HALF + c * W, W)], xv.at[c, h], load_sem.at[2 * c + h]
            )
            cp.start()
            loads.append(cp)
    load_h = pltpu.make_async_copy(h_hbm, hv, load_sem.at[2 * CH])
    load_q = pltpu.make_async_copy(q_hbm, qv, load_sem.at[2 * CH + 1])
    load_h.start()
    load_q.start()

    row = lax.broadcasted_iota(jnp.int32, (2 * NE * SLOT, 1), 0)
    lane = lax.broadcasted_iota(jnp.int32, (2 * NE * SLOT, NE), 1)
    mine = lane == row // (2 * SLOT)
    slot = lax.broadcasted_iota(jnp.int32, (SLOT, NE), 0)
    live_gate = jnp.where(slot < valid_ref[...], gate_ref[...], 0.0)
    local = (idx_ref[...] - e * TOK).astype(F32)

    def column(small):
        tall = jnp.concatenate([small] * (2 * NE), axis=0)
        return jnp.sum(jnp.where(mine, tall, 0.0), axis=1, keepdims=True)

    gates = column(live_gate)
    half_of = lax.rem(row // SLOT, 2)
    token = lax.broadcasted_iota(jnp.int32, (2 * NE * SLOT, TOK), 1).astype(F32)
    hit = token == column(local)
    pick = [
        jnp.where(jnp.logical_and(hit, half_of == h), 1.0, 0.0).astype(BF16) for h in range(2)
    ]

    for c in range(CH):
        loads[2 * c].wait()
        loads[2 * c + 1].wait()
        got = jnp.dot(pick[0], xv[c, 0], preferred_element_type=F32)
        got += jnp.dot(pick[1], xv[c, 1], preferred_element_type=F32)
        routed = (got * gates).astype(BF16)
        sbuf[c] = routed.reshape(NE, 2 * SLOT, W)
        if c == 0:
            pl.semaphore_wait(barrier, NE - 1 + NR - 1)

        def send_rows(i, carry, c=c):
            to = expert_peer(i)
            pltpu.make_async_remote_copy(
                src_ref=sbuf.at[c, to], dst_ref=rbuf.at[c, e], send_sem=row_s.at[c],
                recv_sem=row_r.at[c], device_id=(to, r), device_id_type=MESH,
            ).start()
            return carry

        lax.fori_loop(0, NE - 1, send_rows, 0)
        rbuf[c, e] = sbuf[c, e]

    load_h.wait()
    load_q.wait()
    q_hi, q_rest = split2(qv[...])
    q_mid = q_rest
    q_lo = (qv[...] - q_hi.astype(F32) - q_mid.astype(F32)).astype(BF16)
    hq = dot_nt(hv[...], jnp.concatenate([q_hi, q_mid, q_lo], axis=0))
    hq = hq[:, :RANK] + hq[:, RANK : 2 * RANK] + hq[:, 2 * RANK :]
    hq = hq.reshape(NE, 1, SLOT, RANK)
    hq = jnp.concatenate([hq, hq], axis=1).reshape(2 * NE * SLOT, RANK)
    spread = jnp.concatenate([jnp.where(half_of == h, hq, 0.0) for h in range(2)], axis=1)
    s_hi = spread.astype(BF16).astype(F32)
    left = jnp.concatenate([s_hi, spread - s_hi], axis=1).T.astype(BF16)

    def wait_rows(c):
        some = pl.ds(0, NE - 1)
        pltpu.make_async_copy(sbuf.at[c, some], rbuf.at[c, some], row_r.at[c]).wait()

    def rows(c):
        return rbuf[c].reshape(2 * NE * SLOT, W)

    def start_sum(c):
        both = jnp.dot(left, rows(c), preferred_element_type=F32)
        part = both[: 2 * RANK] + both[2 * RANK :]
        for s in range(8):
            for l in range(4):
                psend[c, s * 4 + l] = part[s * 8 : s * 8 + 8, l * 128 : l * 128 + 128]

        def send(i, carry):
            to = replica_peer(i)
            pltpu.make_async_remote_copy(
                src_ref=psend.at[c, to], dst_ref=prs.at[c, r], send_sem=prs_s.at[c],
                recv_sem=prs_r.at[c], device_id=(e, to), device_id_type=MESH,
            ).start()
            return carry

        lax.fori_loop(0, NR - 1, send, 0)
        prs[c, r] = psend[c, r]

    others = pl.ds(0, NR - 1)

    def start_spread(c):
        pltpu.make_async_copy(psend.at[c, others], prs.at[c, others], prs_r.at[c]).wait()
        pag[c, r] = jnp.sum(prs[c], axis=0)

        def send(i, carry):
            to = replica_peer(i)
            pltpu.make_async_remote_copy(
                src_ref=pag.at[c, r], dst_ref=pag.at[c, r], send_sem=pag_s.at[c],
                recv_sem=pag_r.at[c], device_id=(e, to), device_id_type=MESH,
            ).start()
            return carry

        lax.fori_loop(0, NR - 1, send, 0)

    def factor(c):
        tiles = [
            jnp.concatenate([pag[c, s * 4 + l] for l in range(4)], axis=1) for s in range(8)
        ]
        return jnp.concatenate(tiles, axis=0)

    def take(c, sums):
        pltpu.make_async_copy(prs.at[c, others], pag.at[c, others], pag_r.at[c]).wait()
        hi, lo = split2(factor(c))
        both = jnp.concatenate([hi, lo], axis=0)
        t, g = dot_nt(rows(c), both), dot_nt(both, both)
        return (t, g) if sums is None else (sums[0] + t, sums[1] + g)

    sums = None
    for c in range(CH):
        wait_rows(c)
        start_sum(c)
        if c >= 2:
            sums = take(c - 2, sums)
        if c >= 1:
            start_spread(c - 1)
    sums = take(CH - 2, sums)
    start_spread(CH - 1)
    t, g = take(CH - 1, sums)

    t = (t[:, : 2 * RANK] + t[:, 2 * RANK :]).reshape(NE, 2, SLOT, 2 * RANK)
    t = t[:, 0, :, :RANK] + t[:, 1, :, RANK:]
    t = t.reshape(NE * SLOT, RANK)
    t_hi = t.astype(BF16).astype(F32)
    t = jnp.concatenate([t_hi, t - t_hi], axis=1).T.astype(BF16)
    part = jnp.dot(t, hv[...], preferred_element_type=F32)
    part = part[:RANK] + part[RANK:]
    for s in range(2):
        for l in range(12):
            qsend[s * 12 + l] = part[s * 16 : s * 16 + 16, l * 128 : l * 128 + 128]

    def send_q(i, carry):
        to = replica_peer(i)

        @pl.when(to < QOWN)
        def _():
            pltpu.make_async_remote_copy(
                src_ref=qsend.at[to], dst_ref=qrs.at[r], send_sem=qrs_s.at[0],
                recv_sem=qrs_r.at[0], device_id=(e, to), device_id_type=MESH,
            ).start()

        return carry

    lax.fori_loop(0, NR - 1, send_q, 0)

    g = g[: 2 * RANK] + g[2 * RANK :]
    g = g[:, : 2 * RANK] + g[:, 2 * RANK :]
    g = g[:RANK, :RANK] + g[RANK:, RANK:]
    at_row = lax.broadcasted_iota(jnp.int32, (RANK, RANK), 0)
    at_col = lax.broadcasted_iota(jnp.int32, (RANK, RANK), 1)
    eye = at_row == at_col
    work = jnp.concatenate([g, jnp.where(eye, 1.0, 0.0)], axis=1)
    below = lax.broadcasted_iota(jnp.int32, (RANK, 1), 0)
    for j in range(RANK - 1):
        pivot_row = work[j : j + 1, :]
        scale = work[:, j : j + 1] / pivot_row[:, j : j + 1]
        work = work - jnp.where(below > j, scale, 0.0) * pivot_row
    pivots = jnp.sum(jnp.where(eye, work[:, :RANK], 0.0), axis=1, keepdims=True)
    inverse = work[:, RANK:] / jnp.sqrt(pivots)

    @pl.when(r < QOWN)
    def _():
        pltpu.make_async_copy(qrs.at[others], qrs.at[others], qrs_r.at[0]).wait()
        qrs[r] = qsend[r]
        qag[r] = jnp.sum(qrs[...], axis=0)

        def send(i, carry):
            to = replica_peer(i)
            pltpu.make_async_remote_copy(
                src_ref=qag.at[r], dst_ref=qag.at[r], send_sem=qag_s.at[0],
                recv_sem=qag_r.at[0], device_id=(e, to), device_id_type=MESH,
            ).start()
            return carry

        lax.fori_loop(0, NR - 1, send, 0)

    def solve(mat):
        return jnp.dot(inverse, mat, precision=lax.Precision.HIGHEST, preferred_element_type=F32)

    for c in range(CH):
        fac = factor(c) * math.sqrt(D)
        for h in range(2):
            p_out[:, h * HALF + c * W : h * HALF + c * W + W] = solve(
                fac[h * RANK : h * RANK + RANK]
            )

    @pl.when(r < QOWN)
    def _():
        some = pl.ds(0, QOWN - 1)
        pltpu.make_async_copy(qsend.at[some], qag.at[some], qag_r.at[0]).wait()

    @pl.when(r >= QOWN)
    def _():
        pltpu.make_async_copy(qsend, qag, qag_r.at[0]).wait()

    summed = [
        jnp.concatenate([qag[s * 12 + l] for l in range(12)], axis=1) for s in range(2)
    ]
    q_out[...] = solve(jnp.concatenate(summed, axis=0))

    for c in range(CH):
        some = pl.ds(0, NE - 1)
        pltpu.make_async_copy(sbuf.at[c, some], rbuf.at[c, some], row_s.at[c]).wait()
        pltpu.make_async_copy(psend.at[c, others], prs.at[c, others], prs_s.at[c]).wait()
        pltpu.make_async_copy(psend.at[c, others], prs.at[c, others], pag_s.at[c]).wait()

    @pl.when(r < QOWN)
    def _():
        some = pl.ds(0, QOWN - 1)
        pltpu.make_async_copy(qsend.at[some], qag.at[some], qrs_s.at[0]).wait()
        pltpu.make_async_copy(qrs.at[others], qrs.at[others], qag_s.at[0]).wait()

    @pl.when(r >= QOWN)
    def _():
        pltpu.make_async_copy(qsend, qag, qrs_s.at[0]).wait()


def shards(out_grad, hidden, token_index, router_gate, valid_count, q_previous):
    vmem = pl.BlockSpec(memory_space=pltpu.VMEM)
    hbm = pl.BlockSpec(memory_space=pl.ANY)
    dma = pltpu.SemaphoreType.DMA
    p_t, q_t = pl.pallas_call(
        body,
        name="moe_powersgd",
        out_shape=(
            jax.ShapeDtypeStruct((RANK, D), F32),
            jax.ShapeDtypeStruct((RANK, F), F32),
        ),
        in_specs=[hbm, hbm, hbm, vmem, vmem, vmem],
        out_specs=(vmem, vmem),
        scratch_shapes=[
            pltpu.VMEM((CH, 2, TOK, W), BF16),
            pltpu.VMEM((NE * SLOT, F), BF16),
            pltpu.VMEM((RANK, F), F32),
            pltpu.VMEM((CH, NE, 2 * SLOT, W), BF16),
            pltpu.VMEM((CH, NE, 2 * SLOT, W), BF16),
            pltpu.VMEM((CH, NR, 8, 128), F32),
            pltpu.VMEM((CH, NR, 8, 128), F32),
            pltpu.VMEM((CH, NR, 8, 128), F32),
            pltpu.VMEM((QOWN, 16, 128), F32),
            pltpu.VMEM((NR, 16, 128), F32),
            pltpu.VMEM((QOWN, 16, 128), F32),
            dma((2 * CH + 2,)),
            dma((CH,)), dma((CH,)), dma((CH,)), dma((CH,)), dma((CH,)), dma((CH,)),
            dma((1,)), dma((1,)), dma((1,)), dma((1,)),
        ],
        compiler_params=pltpu.CompilerParams(
            collective_id=0, has_side_effects=True, vmem_limit_bytes=32 << 20
        ),
        cost_estimate=pl.CostEstimate(flops=1 << 30, bytes_accessed=4 << 20, transcendentals=0),
    )(
        out_grad[0],
        hidden[0, 0],
        q_previous[0].T,
        token_index[0].T,
        router_gate[0].T,
        valid_count[0].T,
    )
    return p_t.T[None], q_t.T[None]


def solution(mesh):
    placed = (
        P("replica", "expert", None),
        P("replica", "expert", None, None),
        P("replica", None, "expert"),
        P("replica", None, "expert"),
        P("replica", None, "expert"),
        P("expert", None, None),
    )
    return jax.shard_map(
        shards,
        mesh=mesh,
        in_specs=placed,
        out_specs=(P("expert", None, None), P("expert", None, None)),
        check_vma=False,
    )
```

```python
import math

import jax
import jax.numpy as jnp
from jax import lax
from jax.experimental import pallas as pl
from jax.experimental.pallas import tpu as pltpu
from jax.sharding import PartitionSpec as P

MESH = pl.DeviceIdType.MESH
F32, BF16 = jnp.float32, jnp.bfloat16

D, F, RANK, SLOT, TOK = 4096, 1536, 32, 8, 256
NE, NR = 16, 32
NX, NZ, NY = 4, 8, 8
CH = 4
HALF = D // 2
W = HALF // CH
TL = W // 4
QT, QG = BF16, F32
QOWN = 24


def split2(v):
    hi = v.astype(BF16)
    return hi, (v - hi.astype(F32)).astype(BF16)


def far_first(i, n):
    return lax.rem(n // 2 + (1 - 2 * lax.rem(i, 2)) * ((i + 1) // 2) + n, n)


def dot_nt(a, b):
    return lax.dot_general(a, b, (((1,), (1,)), ((), ())), preferred_element_type=F32)


def body(
    x_hbm, h_hbm, q_hbm, idx_hbm, gate_hbm, valid_hbm,
    p_out, q_out,
    idx_ref, gate_ref, valid_ref,
    xv, hv, qv, sbuf, rbuf, psend, prs, pag, qsend, qrs, qag,
    load_sem, row_s, row_r, prs_s, prs_r, pag_s, pag_r, qrs_s, qrs_r, qag_s, qag_r, meet,
):
    e = lax.axis_index("expert")
    r = lax.axis_index("replica")
    y, core = e // 2, lax.rem(e, 2)
    gx, gz = r // NZ, lax.rem(r, NZ)

    def expert_peer(i):
        to = lax.rem(y + far_first(i // 2, NY), NY)
        return to * 2 + lax.rem(core + 1 - lax.rem(i, 2), 2)

    def replica_peer(i):
        to_z = lax.rem(gz + far_first(i // NX, NZ), NZ)
        to_x = lax.rem(gx + far_first(lax.rem(i, NX), NX), NX)
        return to_x * NZ + to_z

    small = [
        pltpu.make_async_copy(src, dst, load_sem.at[2 * CH + 2 + i])
        for i, (src, dst) in enumerate(
            [(idx_hbm, idx_ref), (gate_hbm, gate_ref), (valid_hbm, valid_ref)]
        )
    ]
    for cp in small:
        cp.start()
    loads = []
    for c in range(CH):
        for h in range(2):
            cp = pltpu.make_async_copy(
                x_hbm.at[:, pl.ds(h * HALF + c * W, W)], xv.at[c, h], load_sem.at[2 * c + h]
            )
            cp.start()
            loads.append(cp)
    load_h = pltpu.make_async_copy(h_hbm, hv, load_sem.at[2 * CH])
    load_q = pltpu.make_async_copy(q_hbm, qv, load_sem.at[2 * CH + 1])
    load_h.start()
    load_q.start()

    barrier = pltpu.get_barrier_semaphore()

    def greet_e(i, c):
        pl.semaphore_signal(barrier, inc=1, device_id=(expert_peer(i), r), device_id_type=MESH)
        return c

    lax.fori_loop(0, NE - 1, greet_e, 0)

    def at(dx, dz):
        return (e, lax.rem(gx + dx + NX, NX) * NZ + lax.rem(gz + dz + NZ, NZ))

    near_z, far_z, near_x = (
        [at(0, 1), at(0, -1)], [at(0, 2), at(0, -2)], [at(1, 0), at(-1, 0)],
    )
    for to in near_z + near_x:
        pl.semaphore_signal(barrier, inc=1, device_id=to, device_id_type=MESH)

    def meet_replicas():
        for step, peers in enumerate([near_z, far_z, near_x, near_x]):
            for to in peers:
                pl.semaphore_signal(meet.at[step], inc=1, device_id=to, device_id_type=MESH)
            pl.semaphore_wait(meet.at[step], 2)

    for cp in small:
        cp.wait()

    row = lax.broadcasted_iota(jnp.int32, (2 * NE * SLOT, 1), 0)
    lane = lax.broadcasted_iota(jnp.int32, (2 * NE * SLOT, NE), 1)
    mine = lane == row // (2 * SLOT)
    slot = lax.broadcasted_iota(jnp.int32, (SLOT, NE), 0)
    live_gate = jnp.where(slot < valid_ref[...], gate_ref[...], 0.0)
    local = (idx_ref[...] - e * TOK).astype(F32)

    def column(small):
        tall = jnp.concatenate([small] * (2 * NE), axis=0)
        return jnp.sum(jnp.where(mine, tall, 0.0), axis=1, keepdims=True)

    gates = column(live_gate)
    half_of = lax.rem(row // SLOT, 2)
    token = lax.broadcasted_iota(jnp.int32, (2 * NE * SLOT, TOK), 1).astype(F32)
    hit = token == column(local)
    pick = [
        jnp.where(jnp.logical_and(hit, half_of == h), 1.0, 0.0).astype(BF16) for h in range(2)
    ]

    for c in range(CH):
        loads[2 * c].wait()
        loads[2 * c + 1].wait()
        got = jnp.dot(pick[0], xv[c, 0], preferred_element_type=F32)
        got += jnp.dot(pick[1], xv[c, 1], preferred_element_type=F32)
        routed = (got * gates).astype(BF16)
        sbuf[c] = routed.reshape(NE, 2 * SLOT, W)
        if c == 0:
            pl.semaphore_wait(barrier, NE - 1 + 4)

        def send_rows(i, carry, c=c):
            to = expert_peer(i)
            pltpu.make_async_remote_copy(
                src_ref=sbuf.at[c, to], dst_ref=rbuf.at[c, e], send_sem=row_s.at[c],
                recv_sem=row_r.at[c], device_id=(to, r), device_id_type=MESH,
            ).start()
            return carry

        lax.fori_loop(0, NE - 1, send_rows, 0)
        rbuf[c, e] = sbuf[c, e]

    meet_replicas()

    load_h.wait()
    load_q.wait()
    q_hi, q_rest = split2(qv[...])
    q_mid = q_rest
    q_lo = (qv[...] - q_hi.astype(F32) - q_mid.astype(F32)).astype(BF16)
    hq = dot_nt(hv[...], jnp.concatenate([q_hi, q_mid, q_lo], axis=0))
    hq = hq[:, :RANK] + hq[:, RANK : 2 * RANK] + hq[:, 2 * RANK :]
    hq = hq.reshape(NE, 1, SLOT, RANK)
    hq = jnp.concatenate([hq, hq], axis=1).reshape(2 * NE * SLOT, RANK)
    spread = jnp.concatenate([jnp.where(half_of == h, hq, 0.0) for h in range(2)], axis=1)
    s_hi = spread.astype(BF16).astype(F32)
    left = jnp.concatenate([s_hi, spread - s_hi], axis=1).T.astype(BF16)

    def wait_rows(c):
        some = pl.ds(0, NE - 1)
        pltpu.make_async_copy(sbuf.at[c, some], rbuf.at[c, some], row_r.at[c]).wait()

    def rows(c):
        return rbuf[c].reshape(2 * NE * SLOT, W)

    def start_sum(c):
        both = jnp.dot(left, rows(c), preferred_element_type=F32)
        part = both[: 2 * RANK] + both[2 * RANK :]
        for s in range(8):
            for l in range(4):
                psend[c, s * 4 + l] = part[s * 8 : s * 8 + 8, l * TL : l * TL + TL]

        def send(i, carry):
            to = replica_peer(i)
            pltpu.make_async_remote_copy(
                src_ref=psend.at[c, to], dst_ref=prs.at[c, r], send_sem=prs_s.at[c],
                recv_sem=prs_r.at[c], device_id=(e, to), device_id_type=MESH,
            ).start()
            return carry

        lax.fori_loop(0, NR - 1, send, 0)
        prs[c, r] = psend[c, r]

    others, owned = pl.ds(0, NR - 1), pl.ds(0, QOWN)

    def start_spread(c):
        pltpu.make_async_copy(psend.at[c, others], prs.at[c, others], prs_r.at[c]).wait()
        pag[c, r] = jnp.sum(prs[c], axis=0)

        def send(i, carry):
            to = replica_peer(i)
            pltpu.make_async_remote_copy(
                src_ref=pag.at[c, r], dst_ref=pag.at[c, r], send_sem=pag_s.at[c],
                recv_sem=pag_r.at[c], device_id=(e, to), device_id_type=MESH,
            ).start()
            return carry

        lax.fori_loop(0, NR - 1, send, 0)

    def factor(c):
        tiles = [
            jnp.concatenate([pag[c, s * 4 + l] for l in range(4)], axis=1) for s in range(8)
        ]
        return jnp.concatenate(tiles, axis=0)

    def take(c, sums):
        pltpu.make_async_copy(prs.at[c, others], pag.at[c, others], pag_r.at[c]).wait()
        hi, lo = split2(factor(c))
        both = jnp.concatenate([hi, lo], axis=0)
        t, g = dot_nt(rows(c), both), dot_nt(both, both)
        return (t, g) if sums is None else (sums[0] + t, sums[1] + g)

    sums = None
    for c in range(CH):
        wait_rows(c)
        start_sum(c)
        if c >= 2:
            sums = take(c - 2, sums)
        if c >= 1:
            start_spread(c - 1)
    start_spread(CH - 1)
    if CH > 1:
        sums = take(CH - 2, sums)
    t, g = take(CH - 1, sums)

    t = (t[:, : 2 * RANK] + t[:, 2 * RANK :]).reshape(NE, 2, SLOT, 2 * RANK)
    t = t[:, 0, :, :RANK] + t[:, 1, :, RANK:]
    t = t.reshape(NE * SLOT, RANK)
    t_hi = t.astype(BF16).astype(F32)
    t = jnp.concatenate([t_hi, t - t_hi], axis=1).T.astype(BF16)
    part = jnp.dot(t, hv[...], preferred_element_type=F32)
    part = part[:RANK] + part[RANK:]
    for s in range(2):
        for l in range(12):
            qsend[s * 12 + l] = part[s * 16 : s * 16 + 16, l * 128 : l * 128 + 128].astype(QT)

    def send_q(i, carry):
        to = replica_peer(i)

        @pl.when(to < QOWN)
        def _():
            pltpu.make_async_remote_copy(
                src_ref=qsend.at[to], dst_ref=qrs.at[r], send_sem=qrs_s.at[0],
                recv_sem=qrs_r.at[0], device_id=(e, to), device_id_type=MESH,
            ).start()

        return carry

    lax.fori_loop(0, NR - 1, send_q, 0)

    g = g[: 2 * RANK] + g[2 * RANK :]
    g = g[:, : 2 * RANK] + g[:, 2 * RANK :]
    g = g[:RANK, :RANK] + g[RANK:, RANK:]
    at_row = lax.broadcasted_iota(jnp.int32, (RANK, RANK), 0)
    at_col = lax.broadcasted_iota(jnp.int32, (RANK, RANK), 1)
    eye = at_row == at_col
    work = jnp.concatenate([g, jnp.where(eye, 1.0, 0.0)], axis=1)
    below = lax.broadcasted_iota(jnp.int32, (RANK, 1), 0)
    for j in range(RANK - 1):
        pivot_row = work[j : j + 1, :]
        scale = work[:, j : j + 1] / pivot_row[:, j : j + 1]
        work = work - jnp.where(below > j, scale, 0.0) * pivot_row
    pivots = jnp.sum(jnp.where(eye, work[:, :RANK], 0.0), axis=1, keepdims=True)
    inverse = work[:, RANK:] / jnp.sqrt(pivots)

    @pl.when(r < QOWN)
    def _():
        pltpu.make_async_copy(qrs.at[others], qrs.at[others], qrs_r.at[0]).wait()
        qrs[r] = qsend[r]
        qag[r] = jnp.sum(qrs[...].astype(F32), axis=0).astype(QG)

        def send(i, carry):
            to = replica_peer(i)
            pltpu.make_async_remote_copy(
                src_ref=qag.at[r], dst_ref=qag.at[r], send_sem=qag_s.at[0],
                recv_sem=qag_r.at[0], device_id=(e, to), device_id_type=MESH,
            ).start()
            return carry

        lax.fori_loop(0, NR - 1, send, 0)

    def solve(mat):
        return jnp.dot(inverse, mat, precision=lax.Precision.HIGHEST, preferred_element_type=F32)

    for c in range(CH):
        fac = factor(c) * math.sqrt(D)
        for h in range(2):
            p_out[:, h * HALF + c * W : h * HALF + c * W + W] = solve(
                fac[h * RANK : h * RANK + RANK]
            )

    @pl.when(r < QOWN)
    def _():
        some = pl.ds(0, QOWN - 1)
        pltpu.make_async_copy(qag.at[some], qag.at[some], qag_r.at[0]).wait()

    @pl.when(r >= QOWN)
    def _():
        pltpu.make_async_copy(qag.at[owned], qag.at[owned], qag_r.at[0]).wait()

    summed = [
        jnp.concatenate([qag[s * 12 + l].astype(F32) for l in range(12)], axis=1)
        for s in range(2)
    ]
    q_out[...] = solve(jnp.concatenate(summed, axis=0))

    for c in range(CH):
        some = pl.ds(0, NE - 1)
        pltpu.make_async_copy(sbuf.at[c, some], rbuf.at[c, some], row_s.at[c]).wait()
        pltpu.make_async_copy(psend.at[c, others], prs.at[c, others], prs_s.at[c]).wait()
        pltpu.make_async_copy(psend.at[c, others], prs.at[c, others], pag_s.at[c]).wait()

    @pl.when(r < QOWN)
    def _():
        some = pl.ds(0, QOWN - 1)
        pltpu.make_async_copy(qsend.at[some], qsend.at[some], qrs_s.at[0]).wait()
        pltpu.make_async_copy(qag.at[others], qag.at[others], qag_s.at[0]).wait()

    @pl.when(r >= QOWN)
    def _():
        pltpu.make_async_copy(qsend, qsend, qrs_s.at[0]).wait()


def shards(out_grad, hidden, token_index, router_gate, valid_count, q_previous):
    vmem = pl.BlockSpec(memory_space=pltpu.VMEM)
    hbm = pl.BlockSpec(memory_space=pl.ANY)
    dma = pltpu.SemaphoreType.DMA
    p_t, q_t = pl.pallas_call(
        body,
        name="moe_powersgd",
        out_shape=(
            jax.ShapeDtypeStruct((RANK, D), F32),
            jax.ShapeDtypeStruct((RANK, F), F32),
        ),
        in_specs=[hbm] * 6,
        out_specs=(vmem, vmem),
        scratch_shapes=[
            pltpu.VMEM((SLOT, NE), jnp.int32),
            pltpu.VMEM((SLOT, NE), F32),
            pltpu.VMEM((1, NE), jnp.int32),
            pltpu.VMEM((CH, 2, TOK, W), BF16),
            pltpu.VMEM((NE * SLOT, F), BF16),
            pltpu.VMEM((RANK, F), F32),
            pltpu.VMEM((CH, NE, 2 * SLOT, W), BF16),
            pltpu.VMEM((CH, NE, 2 * SLOT, W), BF16),
            pltpu.VMEM((CH, NR, 8, TL), F32),
            pltpu.VMEM((CH, NR, 8, TL), F32),
            pltpu.VMEM((CH, NR, 8, TL), F32),
            pltpu.VMEM((QOWN, 16, 128), QT),
            pltpu.VMEM((NR, 16, 128), QT),
            pltpu.VMEM((NR, 16, 128), QG),
            dma((2 * CH + 5,)),
            dma((CH,)), dma((CH,)), dma((CH,)), dma((CH,)), dma((CH,)), dma((CH,)),
            dma((1,)), dma((1,)), dma((1,)), dma((1,)),
            pltpu.SemaphoreType.REGULAR((4,)),
        ],
        compiler_params=pltpu.CompilerParams(
            collective_id=0, has_side_effects=True, vmem_limit_bytes=60 << 20
        ),
        cost_estimate=pl.CostEstimate(flops=1 << 30, bytes_accessed=4 << 20, transcendentals=0),
    )(
        out_grad[0],
        hidden[0, 0],
        q_previous[0].T,
        token_index[0].T,
        router_gate[0].T,
        valid_count[0].T,
    )
    return p_t.T[None], q_t.T[None]


def solution(mesh):
    placed = (
        P("replica", "expert", None),
        P("replica", "expert", None, None),
        P("replica", None, "expert"),
        P("replica", None, "expert"),
        P("replica", None, "expert"),
        P("expert", None, None),
    )
    return jax.shard_map(
        shards,
        mesh=mesh,
        in_specs=placed,
        out_specs=(P("expert", None, None), P("expert", None, None)),
        check_vma=False,
    )
```

```python
import math

import jax
import jax.numpy as jnp
from jax import lax
from jax.experimental import pallas as pl
from jax.experimental.pallas import tpu as pltpu
from jax.sharding import PartitionSpec as P

MESH = pl.DeviceIdType.MESH
F32, BF16 = jnp.float32, jnp.bfloat16

D, F, RANK, SLOT, TOK = 4096, 1536, 32, 8, 256
NE, NR = 16, 32
NX, NZ, NY = 4, 8, 8
CH = 4
HALF = D // 2
W = HALF // CH
TL = W // 4
POWN = NR // 2
QT, QG = BF16, F32
QOWN = 24


def split2(v):
    hi = v.astype(BF16)
    return hi, (v - hi.astype(F32)).astype(BF16)


def far_first(i, n):
    return lax.rem(n // 2 + (1 - 2 * lax.rem(i, 2)) * ((i + 1) // 2) + n, n)


def dot_nt(a, b):
    return lax.dot_general(a, b, (((1,), (1,)), ((), ())), preferred_element_type=F32)


def exact_dot(a, b):
    return jnp.dot(a, b, precision=lax.Precision.HIGHEST, preferred_element_type=F32)


def finish(p_hbm, q_hbm, inv_hbm, p_out, q_out, pv, qv, iv, qo, sem_in, sem_out):
    small = [
        pltpu.make_async_copy(inv_hbm, iv, sem_in.at[CH]),
        pltpu.make_async_copy(q_hbm, qv, sem_in.at[CH + 1]),
    ]
    wide = [pl.ds(c * (D // CH), D // CH) for c in range(CH)]
    ins = [pltpu.make_async_copy(p_hbm.at[:, wide[c]], pv.at[c], sem_in.at[c]) for c in range(CH)]
    outs = [pltpu.make_async_copy(pv.at[c], p_out.at[:, wide[c]], sem_out.at[c]) for c in range(CH)]
    for cp in small + ins:
        cp.start()
    for cp in small:
        cp.wait()
    qo[...] = exact_dot(iv[...], qv[...])
    last = pltpu.make_async_copy(qo, q_out, sem_out.at[CH])
    last.start()
    for c in range(CH):
        ins[c].wait()
        outs[c].start()
    for cp in outs + [last]:
        cp.wait()


def body(
    x_hbm, h_hbm, q_hbm, idx_hbm, gate_hbm, valid_hbm,
    p_hbm, q_out, inv_out,
    idx_ref, gate_ref, valid_ref,
    xv, hv, qv, sbuf, rbuf, psend, prs, pag, sent, qsend, qrs, qag, p_out, hdup,
    load_sem, row_s, row_r, prs_s, prs_r, pag_s, pag_r, qrs_s, qrs_r, qag_s, qag_r, meet,
):
    e = lax.axis_index("expert")
    r = lax.axis_index("replica")
    y, core = e // 2, lax.rem(e, 2)
    gx, gz = r // NZ, lax.rem(r, NZ)

    def expert_peer(i):
        to = lax.rem(y + far_first(i // 2, NY), NY)
        return to * 2 + lax.rem(core + 1 - lax.rem(i, 2), 2)

    def replica_peer(i):
        to_z = lax.rem(gz + far_first(i // NX, NZ), NZ)
        to_x = lax.rem(gx + far_first(lax.rem(i, NX), NX), NX)
        return to_x * NZ + to_z

    small = [
        pltpu.make_async_copy(src, dst, load_sem.at[2 * CH + 2 + i])
        for i, (src, dst) in enumerate(
            [(idx_hbm, idx_ref), (gate_hbm, gate_ref), (valid_hbm, valid_ref)]
        )
    ]
    for cp in small:
        cp.start()
    loads = []
    for c in range(CH):
        for h in range(2):
            cp = pltpu.make_async_copy(
                x_hbm.at[:, pl.ds(h * HALF + c * W, W)], xv.at[c, h], load_sem.at[2 * c + h]
            )
            cp.start()
            loads.append(cp)
    load_h = pltpu.make_async_copy(h_hbm, hv, load_sem.at[2 * CH])
    load_q = pltpu.make_async_copy(q_hbm, qv, load_sem.at[2 * CH + 1])
    load_h.start()
    load_q.start()

    barrier = pltpu.get_barrier_semaphore()

    def greet_e(i, c):
        pl.semaphore_signal(barrier, inc=1, device_id=(expert_peer(i), r), device_id_type=MESH)
        return c

    lax.fori_loop(0, NE - 1, greet_e, 0)

    def at(dx, dz):
        return (e, lax.rem(gx + dx + NX, NX) * NZ + lax.rem(gz + dz + NZ, NZ))

    near_z, far_z, near_x = (
        [at(0, 1), at(0, -1)], [at(0, 2), at(0, -2)], [at(1, 0), at(-1, 0)],
    )
    for to in near_z + near_x:
        pl.semaphore_signal(barrier, inc=1, device_id=to, device_id_type=MESH)

    def meet_replicas():
        for step, peers in enumerate([near_z, far_z, near_x, near_x]):
            for to in peers:
                pl.semaphore_signal(meet.at[step], inc=1, device_id=to, device_id_type=MESH)
            pl.semaphore_wait(meet.at[step], 2)

    for cp in small:
        cp.wait()

    row = lax.broadcasted_iota(jnp.int32, (2 * NE * SLOT, 1), 0)
    lane = lax.broadcasted_iota(jnp.int32, (2 * NE * SLOT, NE), 1)
    mine = lane == row // (2 * SLOT)
    slot = lax.broadcasted_iota(jnp.int32, (SLOT, NE), 0)
    live_gate = jnp.where(slot < valid_ref[...], gate_ref[...], 0.0)
    local = (idx_ref[...] - e * TOK).astype(F32)

    def column(small):
        tall = jnp.concatenate([small] * (2 * NE), axis=0)
        return jnp.sum(jnp.where(mine, tall, 0.0), axis=1, keepdims=True)

    gates = column(live_gate)
    half_of = lax.rem(row // SLOT, 2)
    token = lax.broadcasted_iota(jnp.int32, (2 * NE * SLOT, TOK), 1).astype(F32)
    hit = token == column(local)
    pick = [
        jnp.where(jnp.logical_and(hit, half_of == h), 1.0, 0.0).astype(BF16) for h in range(2)
    ]

    for c in range(CH):
        loads[2 * c].wait()
        loads[2 * c + 1].wait()
        got = jnp.dot(pick[0], xv[c, 0], preferred_element_type=F32)
        got += jnp.dot(pick[1], xv[c, 1], preferred_element_type=F32)
        routed = (got * gates).astype(BF16)
        sbuf[c] = routed.reshape(NE, 2 * SLOT, W)
        if c == 0:
            pl.semaphore_wait(barrier, NE - 1 + 4)

        def send_rows(i, carry, c=c):
            to = expert_peer(i)
            pltpu.make_async_remote_copy(
                src_ref=sbuf.at[c, to], dst_ref=rbuf.at[c, e], send_sem=row_s.at[c],
                recv_sem=row_r.at[c], device_id=(to, r), device_id_type=MESH,
            ).start()
            return carry

        lax.fori_loop(0, NE - 1, send_rows, 0)
        rbuf[c, e] = sbuf[c, e]

    meet_replicas()

    load_h.wait()
    load_q.wait()
    q_hi, q_rest = split2(qv[...])
    q_mid = q_rest
    q_lo = (qv[...] - q_hi.astype(F32) - q_mid.astype(F32)).astype(BF16)
    hq = dot_nt(hv[...], jnp.concatenate([q_hi, q_mid, q_lo], axis=0))
    hq = hq[:, :RANK] + hq[:, RANK : 2 * RANK] + hq[:, 2 * RANK :]
    hq = hq.reshape(NE, 1, SLOT, RANK)
    hq = jnp.concatenate([hq, hq], axis=1).reshape(2 * NE * SLOT, RANK)
    spread = jnp.concatenate([jnp.where(half_of == h, hq, 0.0) for h in range(2)], axis=1)
    s_hi = spread.astype(BF16).astype(F32)
    left = jnp.concatenate([s_hi, spread - s_hi], axis=1).T.astype(BF16)
    twice = hv[...].astype(F32).reshape(NE, 1, SLOT, F)
    twice = jnp.concatenate([twice, twice], axis=1).reshape(2 * NE * SLOT, F)
    hdup[...] = twice.astype(BF16)

    def wait_rows(c):
        some = pl.ds(0, NE - 1)
        pltpu.make_async_copy(sbuf.at[c, some], rbuf.at[c, some], row_r.at[c]).wait()

    def rows(c):
        return rbuf[c].reshape(2 * NE * SLOT, W)

    def start_sum(c):
        both = jnp.dot(left, rows(c), preferred_element_type=F32)
        part = both[: 2 * RANK] + both[2 * RANK :]
        for s in range(4):
            for l in range(4):
                psend[c, s * 4 + l] = part[s * 16 : s * 16 + 16, l * TL : l * TL + TL]
        other = lax.rem(r + c, 2)

        def send(i, carry):
            k = i // NX
            to = replica_peer((2 * k + lax.rem(k + other, 2)) * NX + lax.rem(i, NX))

            @pl.when(to != r)
            def _():
                pltpu.make_async_remote_copy(
                    src_ref=psend.at[c, to // 2], dst_ref=prs.at[c, r], send_sem=prs_s.at[c],
                    recv_sem=prs_r.at[c], device_id=(e, to), device_id_type=MESH,
                ).start()

            return carry

        lax.fori_loop(0, POWN, send, 0)

    others, owned = pl.ds(0, NR - 1), pl.ds(0, QOWN)

    def start_spread(c):
        @pl.when(lax.rem(r + c, 2) == 0)
        def _():
            pltpu.make_async_copy(prs.at[c, others], prs.at[c, others], prs_r.at[c]).wait()
            prs[c, r] = psend[c, r // 2]
            pag[c, r // 2] = jnp.sum(prs[c], axis=0).astype(BF16)

            def send(i, carry):
                to = replica_peer(i)
                pltpu.make_async_remote_copy(
                    src_ref=pag.at[c, r // 2], dst_ref=pag.at[c, r // 2], send_sem=pag_s.at[c],
                    recv_sem=pag_r.at[c], device_id=(e, to), device_id_type=MESH,
                ).start()
                return carry

            lax.fori_loop(0, NR - 1, send, 0)

    def factor(c):
        blocks = [
            jnp.concatenate([pag[c, s * 4 + l] for l in range(4)], axis=1) for s in range(4)
        ]
        return jnp.concatenate(blocks, axis=0)

    def wait_blocks(c, buf, sem):
        @pl.when(lax.rem(r + c, 2) == 0)
        def _():
            some = pl.ds(0, POWN - 1)
            pltpu.make_async_copy(buf.at[c, some], buf.at[c, some], sem.at[c]).wait()

        @pl.when(lax.rem(r + c, 2) == 1)
        def _():
            pltpu.make_async_copy(buf.at[c], buf.at[c], sem.at[c]).wait()

    def take(c, sums):
        wait_blocks(c, pag, pag_r)
        fac = factor(c)
        t, g = dot_nt(fac, rows(c)), dot_nt(fac, fac)
        return (t, g) if sums is None else (sums[0] + t, sums[1] + g)

    sums = None
    for c in range(CH):
        wait_rows(c)
        start_sum(c)
        if c >= 2:
            sums = take(c - 2, sums)
        if c >= 1:
            start_spread(c - 1)
    start_spread(CH - 1)
    if CH > 1:
        sums = take(CH - 2, sums)
    t, g = take(CH - 1, sums)

    at_half = lax.broadcasted_iota(jnp.int32, (2 * RANK, 2 * NE * SLOT), 0) // RANK
    of_half = lax.rem(lax.broadcasted_iota(jnp.int32, at_half.shape, 1) // SLOT, 2)
    t_hi, t_lo = split2(jnp.where(at_half == of_half, t, 0.0))
    part = jnp.dot(
        jnp.concatenate([t_hi, t_lo], axis=0), hdup[...], preferred_element_type=F32
    )
    part = part[: 2 * RANK] + part[2 * RANK :]
    part = part[:RANK] + part[RANK:]
    for s in range(2):
        for l in range(12):
            qsend[s * 12 + l] = part[s * 16 : s * 16 + 16, l * 128 : l * 128 + 128].astype(QT)

    def send_q(i, carry):
        to = replica_peer(i)

        @pl.when(to < QOWN)
        def _():
            pltpu.make_async_remote_copy(
                src_ref=qsend.at[to], dst_ref=qrs.at[r], send_sem=qrs_s.at[0],
                recv_sem=qrs_r.at[0], device_id=(e, to), device_id_type=MESH,
            ).start()

        return carry

    lax.fori_loop(0, NR - 1, send_q, 0)

    g = g[:RANK, :RANK] + g[RANK:, RANK:]
    at_row = lax.broadcasted_iota(jnp.int32, (RANK, RANK), 0)
    at_col = lax.broadcasted_iota(jnp.int32, (RANK, RANK), 1)
    eye = at_row == at_col
    work = jnp.concatenate([g, jnp.where(eye, 1.0, 0.0)], axis=1)
    below = lax.broadcasted_iota(jnp.int32, (RANK, 1), 0)
    for j in range(RANK - 1):
        pivot_row = work[j : j + 1, :]
        scale = work[:, j : j + 1] / pivot_row[:, j : j + 1]
        work = work - jnp.where(below > j, scale, 0.0) * pivot_row
    pivots = jnp.sum(jnp.where(eye, work[:, :RANK], 0.0), axis=1, keepdims=True)
    inverse = work[:, RANK:] / jnp.sqrt(pivots)
    inv_out[...] = inverse

    @pl.when(r < QOWN)
    def _():
        pltpu.make_async_copy(qrs.at[others], qrs.at[others], qrs_r.at[0]).wait()
        qrs[r] = qsend[r]
        qag[r] = jnp.sum(qrs[...].astype(F32), axis=0).astype(QG)

        def send(i, carry):
            to = replica_peer(i)
            pltpu.make_async_remote_copy(
                src_ref=qag.at[r], dst_ref=qag.at[r], send_sem=qag_s.at[0],
                recv_sem=qag_r.at[0], device_id=(e, to), device_id_type=MESH,
            ).start()
            return carry

        lax.fori_loop(0, NR - 1, send, 0)

    for c in range(CH):
        fac = factor(c).astype(F32) * math.sqrt(D)
        for h in range(2):
            p_out[:, h * HALF + c * W : h * HALF + c * W + W] = exact_dot(
                inverse, fac[h * RANK : h * RANK + RANK]
            )

    store_p = pltpu.make_async_copy(p_out, p_hbm, load_sem.at[0])
    store_p.start()

    @pl.when(r < QOWN)
    def _():
        some = pl.ds(0, QOWN - 1)
        pltpu.make_async_copy(qag.at[some], qag.at[some], qag_r.at[0]).wait()

    @pl.when(r >= QOWN)
    def _():
        pltpu.make_async_copy(qag.at[owned], qag.at[owned], qag_r.at[0]).wait()

    summed = [
        jnp.concatenate([qag[s * 12 + l].astype(F32) for l in range(12)], axis=1)
        for s in range(2)
    ]
    q_out[...] = jnp.concatenate(summed, axis=0)

    store_p.wait()
    for c in range(CH):
        some = pl.ds(0, NE - 1)
        pltpu.make_async_copy(sbuf.at[c, some], rbuf.at[c, some], row_s.at[c]).wait()
        wait_blocks(c, psend, prs_s)

        @pl.when(lax.rem(r + c, 2) == 0)
        def _(c=c):
            pltpu.make_async_copy(sent.at[others], sent.at[others], pag_s.at[c]).wait()

    @pl.when(r < QOWN)
    def _():
        some = pl.ds(0, QOWN - 1)
        pltpu.make_async_copy(qsend.at[some], qsend.at[some], qrs_s.at[0]).wait()
        pltpu.make_async_copy(qag.at[others], qag.at[others], qag_s.at[0]).wait()

    @pl.when(r >= QOWN)
    def _():
        pltpu.make_async_copy(qsend, qsend, qrs_s.at[0]).wait()


def shards(out_grad, hidden, token_index, router_gate, valid_count, q_previous):
    vmem = pl.BlockSpec(memory_space=pltpu.VMEM)
    hbm = pl.BlockSpec(memory_space=pl.ANY)
    dma = pltpu.SemaphoreType.DMA
    p_t, q_sum, inverse = pl.pallas_call(
        body,
        name="moe_powersgd",
        out_shape=(
            jax.ShapeDtypeStruct((RANK, D), F32),
            jax.ShapeDtypeStruct((RANK, F), F32),
            jax.ShapeDtypeStruct((RANK, RANK), F32),
        ),
        in_specs=[hbm] * 6,
        out_specs=(hbm, vmem, vmem),
        scratch_shapes=[
            pltpu.VMEM((SLOT, NE), jnp.int32),
            pltpu.VMEM((SLOT, NE), F32),
            pltpu.VMEM((1, NE), jnp.int32),
            pltpu.VMEM((CH, 2, TOK, W), BF16),
            pltpu.VMEM((NE * SLOT, F), BF16),
            pltpu.VMEM((RANK, F), F32),
            pltpu.VMEM((CH, NE, 2 * SLOT, W), BF16),
            pltpu.VMEM((CH, NE, 2 * SLOT, W), BF16),
            pltpu.VMEM((CH, POWN, 16, TL), F32),
            pltpu.VMEM((CH, NR, 16, TL), F32),
            pltpu.VMEM((CH, POWN, 16, TL), BF16),
            pltpu.VMEM((NR, 16, TL), BF16),
            pltpu.VMEM((QOWN, 16, 128), QT),
            pltpu.VMEM((NR, 16, 128), QT),
            pltpu.VMEM((NR, 16, 128), QG),
            pltpu.VMEM((RANK, D), F32),
            pltpu.VMEM((2 * NE * SLOT, F), BF16),
            dma((2 * CH + 5,)),
            dma((CH,)), dma((CH,)), dma((CH,)), dma((CH,)), dma((CH,)), dma((CH,)),
            dma((1,)), dma((1,)), dma((1,)), dma((1,)),
            pltpu.SemaphoreType.REGULAR((4,)),
        ],
        compiler_params=pltpu.CompilerParams(
            collective_id=0, has_side_effects=True, vmem_limit_bytes=60 << 20
        ),
        cost_estimate=pl.CostEstimate(flops=1 << 30, bytes_accessed=4 << 20, transcendentals=0),
    )(
        out_grad[0],
        hidden[0, 0],
        q_previous[0].T,
        token_index[0].T,
        router_gate[0].T,
        valid_count[0].T,
    )
    p_t, q_t = pl.pallas_call(
        finish,
        name="finish",
        out_shape=(
            jax.ShapeDtypeStruct((RANK, D), F32),
            jax.ShapeDtypeStruct((RANK, F), F32),
        ),
        in_specs=[hbm] * 3,
        out_specs=(hbm, hbm),
        scratch_shapes=[
            pltpu.VMEM((CH, RANK, D // CH), F32),
            pltpu.VMEM((RANK, F), F32),
            pltpu.VMEM((RANK, RANK), F32),
            pltpu.VMEM((RANK, F), F32),
            dma((CH + 2,)),
            dma((CH + 1,)),
        ],
        compiler_params=pltpu.CompilerParams(vmem_limit_bytes=60 << 20),
    )(p_t, q_sum, inverse)
    return p_t.T[None], q_t.T[None]


def solution(mesh):
    placed = (
        P("replica", "expert", None),
        P("replica", "expert", None, None),
        P("replica", None, "expert"),
        P("replica", None, "expert"),
        P("replica", None, "expert"),
        P("expert", None, None),
    )
    return jax.shard_map(
        shards,
        mesh=mesh,
        in_specs=placed,
        out_specs=(P("expert", None, None), P("expert", None, None)),
        check_vma=False,
    )
```
